512 devices in a mesh: segment: 4 (over y), expert: 32 (over z, core), cuts: 4 (over x).
Axes of the slice: x: 4, y: 4, z: 16, core: 2. Of those that a mesh axis runs over, the one named last changes fastest.
Arguments:
- activations: bfloat16 [4, 4096, 3072], P('segment', 'expert', 'cuts'), may hold values from -6 to 6
- pred_routes: int32 [4, 4096, 2], P('segment', 'expert'), may hold values from 0 to 7, all different within a row; in each aligned block of 128 rows (0 to 127, 128 to 255, ..., all dimensions but the last counted through in order) at most 48 rows name the same one
- true_routes: int32 [4, 4096, 2], P('segment', 'expert'), may hold values from 0 to 7, all different within a row
- gate_scores: float32 [4, 4096, 2], P('segment', 'expert'), may hold values from 0.05 to 1
- mis_rows: int32 [4, 256], P('segment', 'expert'), may hold values from 0 to 127, as said below
- mis_count: int32 [4, 32], P('segment', 'expert'), may hold values from 4 to 8, as said below
- w_up: bfloat16 [4, 32, 3072, 1024], P('segment', 'expert', 'cuts'), may hold values from -0.109375 to 0.109375
- w_down: bfloat16 [4, 32, 1024, 3072], P('segment', 'expert', None, 'cuts'), may hold values from -0.1875 to 0.1875
Outputs:
- mixed: bfloat16 [4, 4096, 3072], P('segment', 'expert', 'cuts')
The draws below stay inside these ranges and needn't reach their ends.
Inputs may be any that keep to these rules, and one draw needn't show every extreme that they name: `pred_routes`: two different experts a token. In the rows of one device no expert is named more than 48 times, a bound that some block reaches. `true_routes`: two different experts a token. `mis_rows`: the 8 entries of each device are distinct local row indices of its own 128 tokens. `mis_count`: in every section some device uses all 8 entries.
All inputs are finite; a program needn't handle non-finite values.
Results may differ from the reference program's by a relative error of at most 0.017.
Values may be sent and summed in bfloat16 or wider, within the bound.
No kernel may reach another device: no remote copies, remote signals or barrier semaphores. Data moves between devices by JAX's collectives and lax.ppermute only.
A program may use at most 64 MiB of HBM per device.

```python
import math
import jax
import jax.numpy as jnp
import numpy as np
from jax import lax

D = 3072
EXPERTS = 8
TOP = 2
EXP_FLIGHT = 2
FF_DEV = 1024
TOK_DEV = 128
EXPERT_ROW_LIMIT = 48
LISTED_ROW_LIMIT = 8
SEGMENTS = 4
GROUP = 16
TOKENS = 4096
N_EXPERT = 32
N_CUTS = 4


def draw_mis_rows(key, part):
    key = jax.random.fold_in(key, 11)
    holders = SEGMENTS * (TOKENS // TOK_DEV)
    keyset = jax.random.split(key, holders)
    picked = jax.vmap(lambda single: jax.random.permutation(single, TOK_DEV)[:LISTED_ROW_LIMIT])(keyset)
    return picked.reshape(SEGMENTS, TOKENS // TOK_DEV * LISTED_ROW_LIMIT).astype(jnp.int32)


def draw_mis_count(key, part):
    key = jax.random.fold_in(key, 12)
    first_key, second_key = jax.random.split(key)
    holders = TOKENS // TOK_DEV
    counts = jax.random.randint(first_key, (SEGMENTS, holders), LISTED_ROW_LIMIT // 2, LISTED_ROW_LIMIT + 1)
    fullest = jax.random.randint(second_key, (SEGMENTS, 1), 0, holders)
    counts = jnp.where(jnp.arange(holders)[None, :] == fullest, LISTED_ROW_LIMIT, counts)
    return counts.astype(jnp.int32)


def levels(rng, shape, shards, low, top_value):
    factor_of = 1.0
    for axis_at, parts in shards:
        heights = jax.random.uniform(jax.random.fold_in(jax.random.fold_in(rng, 6), axis_at), (parts,), jnp.float32, low / len(shards), top_value / len(shards))
        factor_of = factor_of * jnp.repeat(jnp.exp(heights), shape[axis_at] // parts).reshape((-1,) + (1,) * (len(shape) - 1 - axis_at))
    return factor_of


def choose_distinct(stream_key, rows, amount, top, lift):
    sequence = jax.random.permutation(jax.random.fold_in(stream_key, 1), amount)
    boost = sequence
    for power in range(3):
        boost = boost * boost // amount
    boost = boost * lift // amount
    lots = jax.random.randint(jax.random.fold_in(stream_key, 2), (rows, amount), 0, 4096) + boost
    sure = jax.random.permutation(jax.random.fold_in(stream_key, 3), rows)[jnp.arange(amount) % rows]
    lots = jnp.where(jnp.arange(rows)[:, None] == sure[None, :], 1 << 14, lots)
    merit = lots * amount + jnp.arange(amount)
    return lax.top_k(merit.astype(jnp.int32), top)[1].astype(jnp.int32)


def assign_block(own_key, own, number, rows, count, top, most, lean):
    ranking = jax.random.permutation(own_key, count)
    packed, common = shares(count, rows * top, most, lean, True), shares(count, rows * top, most, lean, False)
    places = jnp.arange(count)

    def named(lengths, rotation):
        used = int((lengths > 0).sum())
        fixed = max(1, used // 4)
        shifted = fixed + (places - fixed + rotation * (used - fixed)) % max(1, count - fixed)
        return jnp.zeros((count,), jnp.int32).at[ranking[jnp.where(places < fixed, places, shifted)]].set(jnp.asarray(lengths, jnp.int32))

    lengths = jnp.where(number % 4 == 0, named(packed, number // 4), named(common, number - number // 4 - 1))
    mixed = jax.random.permutation(jax.random.fold_in(own, 3), count)
    source_of, sink = mixed[0:count // 2 * 2:2], mixed[1:count // 2 * 2:2]
    slack = jnp.minimum(lengths[source_of] - 1, most - lengths[sink]) // 2
    slack = jnp.where((source_of == ranking[0]) | (sink == ranking[0]) | (lengths[sink] == 0), 0, jnp.maximum(slack, 0))
    shifted = jax.random.randint(jax.random.fold_in(own, 4), (count // 2,), 0, 1 << 20) % (slack + 1)
    lengths = lengths.at[source_of].add(-shifted).at[sink].add(shifted)
    labels = jnp.searchsorted(jnp.cumsum(lengths), jnp.arange(rows * top), side="right").astype(jnp.int32)
    table = labels.reshape(top, rows).T
    table = table[jax.random.permutation(jax.random.fold_in(own, 1), rows)]
    rotation = jax.random.randint(jax.random.fold_in(own, 2), (rows, 1), 0, top)
    return jnp.take_along_axis(table, (jnp.arange(top)[None, :] + rotation) % top, axis=1)


def shares(number_of, total, reach, lean, full):
    loads = [(1 << 20) // math.isqrt(grade ** lean) + 1 for grade in range(1, number_of + 1)]
    largest = reach if full else min(reach, max(-(-total // number_of), total * loads[0] // sum(loads)))
    least = 1 if total - largest >= number_of - 1 else 0
    holding, spare = [largest] + [least] * (number_of - 1), total - largest - least * (number_of - 1)
    while spare > 0:
        movable = [i for i in range(1, number_of) if holding[i] < largest] or [i for i in range(1, number_of) if holding[i] < reach]
        pool, left = sum([loads[i] for i in movable]), spare
        for i in movable:
            extra = min(reach - holding[i], max(1, left * loads[i] // pool), spare)
            holding[i] = holding[i] + extra
            spare = spare - extra
    return np.array(holding)


def gaussian(rng, shape, scale, most, pieces=(), kind=jnp.bfloat16):
    array = jax.random.normal(rng, shape, jnp.float32) * scale
    if len(pieces) > 0:
        array = levels(rng, shape, pieces, -0.22, 0.18) * array
    return jnp.clip(array, min=-most, max=most).astype(kind)


def setup_inputs(seed: int = 0) -> dict:
    key_list = jax.random.split(jax.random.key(seed), 9)
    activations = gaussian(key_list[0], (SEGMENTS, TOKENS, D), 1.0, 6.0, ((0, 4), (1, 32), (2, 4)))
    pred_routes_keys = jax.random.split(jax.random.fold_in(key_list[1], 1), SEGMENTS * TOKENS // TOK_DEV)
    pred_routes_turns = jax.random.permutation(jax.random.fold_in(key_list[1], 3), SEGMENTS * TOKENS // TOK_DEV)
    pred_routes = jax.vmap(lambda own, number: assign_block(jax.random.fold_in(key_list[1], 2), own, number, TOK_DEV, EXPERTS, TOP, EXPERT_ROW_LIMIT, 2))(pred_routes_keys, pred_routes_turns).reshape((SEGMENTS, TOKENS, TOP))
    true_routes = choose_distinct(key_list[2], SEGMENTS * TOKENS, EXPERTS, TOP, 2048).reshape((SEGMENTS, TOKENS, TOP))
    gate_scores = jnp.clip(jnp.exp(math.log(1.0) - 2.9957323 * jax.random.uniform(key_list[3], (SEGMENTS, TOKENS, TOP), jnp.float32) ** levels(key_list[3], (SEGMENTS, TOKENS, TOP), ((0, 4), (1, 32)), -0.2, 0.2)), 0.05, 1.0)
    mis_rows = draw_mis_rows(jax.random.fold_in(key_list[8], 71), 0)
    mis_count = draw_mis_count(jax.random.fold_in(key_list[8], 71), 0)
    w_up = gaussian(key_list[6], (SEGMENTS, N_EXPERT, D, FF_DEV), D ** -0.5, 0.109375, ((0, 4), (1, 32), (2, 4)))
    w_down = gaussian(key_list[7], (SEGMENTS, N_EXPERT, FF_DEV, D), FF_DEV ** -0.5, 0.1875, ((0, 4), (1, 32), (3, 4)))
    return dict(activations=activations, pred_routes=pred_routes, true_routes=true_routes, gate_scores=gate_scores, mis_rows=mis_rows, mis_count=mis_count, w_up=w_up, w_down=w_down)


def reference(activations, pred_routes, true_routes, gate_scores, mis_rows, mis_count, w_up, w_down):
    received = jnp.roll(activations, 1, axis=0)
    holders = TOKENS // TOK_DEV
    bound = holders * (EXPERT_ROW_LIMIT + LISTED_ROW_LIMIT)
    width_cut = D // N_CUTS
    results = []
    for segment_idx in range(SEGMENTS):
        positions = jnp.arange(TOKENS, dtype=jnp.int32)
        local_row = positions % TOK_DEV
        holder_of = positions // TOK_DEV
        listing = mis_rows[segment_idx].reshape(holders, LISTED_ROW_LIMIT)
        in_use = jnp.arange(LISTED_ROW_LIMIT, dtype=jnp.int32)[None, :] < mis_count[segment_idx][:, None]
        matches = (listing[holder_of] == local_row[:, None]) & in_use[holder_of]
        listed = jnp.any(matches, axis=1)
        routes = jnp.where(listed[:, None], true_routes[segment_idx], pred_routes[segment_idx])
        scores = gate_scores[segment_idx]
        gate = scores / jnp.sum(scores, axis=1, keepdims=True)
        tokens_in = received[segment_idx]
        mixed = tokens_in.astype(jnp.float32)
        for expert_idx in range(EXP_FLIGHT):
            factor = jnp.sum(jnp.where(routes == expert_idx, gate, 0.0), axis=1)
            chosen = jnp.any(routes == expert_idx, axis=1)
            picked = jnp.nonzero(chosen, size=bound, fill_value=0)[0].astype(jnp.int32)
            number = jnp.sum(chosen.astype(jnp.int32))
            up_slices = w_up[segment_idx, expert_idx * GROUP:(expert_idx + 1) * GROUP]
            up_whole = jnp.transpose(up_slices, (1, 0, 2)).reshape(D, GROUP * FF_DEV)
            down_whole = w_down[segment_idx, expert_idx * GROUP:(expert_idx + 1) * GROUP].reshape(GROUP * FF_DEV, D)
            picked_rows = tokens_in[picked]
            hidden = jnp.zeros((bound, GROUP * FF_DEV), jnp.float32)
            for boundary_index in range(N_CUTS):
                lower = boundary_index * width_cut
                portion = jnp.dot(picked_rows[:, lower:lower + width_cut], up_whole[lower:lower + width_cut], preferred_element_type=jnp.float32)
                rounded = lax.optimization_barrier(portion.astype(jnp.bfloat16))
                hidden = hidden + rounded.astype(jnp.float32)
            active = jax.nn.gelu(hidden).astype(jnp.bfloat16)
            expert_out = jnp.zeros((bound, D), jnp.float32)
            for group_idx in range(GROUP):
                low = group_idx * FF_DEV
                share = jnp.dot(active[:, low:low + FF_DEV], down_whole[low:low + FF_DEV], preferred_element_type=jnp.float32)
                share_rounded = lax.optimization_barrier(share.astype(jnp.bfloat16))
                expert_out = expert_out + share_rounded.astype(jnp.float32)
            alive = jnp.arange(bound, dtype=jnp.int32) < number
            scale_rows = jnp.where(alive, factor[picked], 0.0)
            mixed = mixed.at[picked].add(expert_out * scale_rows[:, None])
        results.append(mixed.astype(jnp.bfloat16))
    return jnp.stack(results)
```

```python
import jax
import jax.numpy as jnp
from jax import lax
from jax.sharding import PartitionSpec as P

EXP_FLIGHT = 2
ROW_LIMIT = 56
CHUNK_GROUPS = ((0,), (3,), (2,), (1,))


def moved(value, axis, targets):
    return lax.ppermute(value, axis, list(enumerate(targets)))


def along_chips(value, by):
    count = lax.axis_size("expert")
    return moved(value, "expert", [(j + 2 * by) % count for j in range(count)])


def swapped_chips(value, mask):
    return moved(value, "expert", [j ^ (2 * mask) for j in range(lax.axis_size("expert"))])


def other_core(value):
    return moved(value, "expert", [j ^ 1 for j in range(lax.axis_size("expert"))])


def along_cuts(value, by):
    count = lax.axis_size("cuts")
    return moved(value, "cuts", [(i + by) % count for i in range(count)])


def cut_sum(blocks):
    from_left = along_cuts(blocks[1], 1)
    from_right = along_cuts(blocks[3], 3)
    from_far = along_cuts(blocks[2], 2)
    return sum(part.astype(jnp.float32) for part in (blocks[0], from_left, from_right, from_far))


def cut_gather(own):
    from_right = along_cuts(own, 3)
    from_far = along_cuts(own, 2)
    from_left = along_cuts(own, 1)
    return [own, from_right, from_far, from_left]


def shards(activations, pred_routes, true_routes, gate_scores, mis_rows, mis_count, w_up, w_down):
    arrived = lax.ppermute(activations, "segment", [(i, (i + 1) % 4) for i in range(4)])[0]
    tok_rows, width = arrived.shape
    up, down = w_up[0, 0], w_down[0, 0]
    chip = lax.axis_index("expert") // 2
    cut = lax.axis_index("cuts")
    half = chip // 8
    low = (chip % 8) < 4

    scores = gate_scores[0]
    gate = scores / jnp.sum(scores, axis=1, keepdims=True)
    listing = mis_rows[0]
    in_use = jnp.arange(listing.shape[0], dtype=jnp.int32) < mis_count[0, 0]
    listed = jnp.any(
        (jnp.arange(tok_rows, dtype=jnp.int32)[:, None] == listing[None, :]) & in_use[None, :],
        axis=1,
    )
    routes = jnp.where(listed[:, None], true_routes[0], pred_routes[0])
    order = jnp.stack([half, 1 - half])
    named = routes[None, :, :] == order[:, None, None]
    chosen = jnp.any(named, axis=2)
    factor = jnp.sum(jnp.where(named, gate[None], 0.0), axis=2)
    before = jnp.arange(tok_rows)[:, None] < jnp.arange(tok_rows)[None, :]
    position = jnp.dot(
        chosen.astype(jnp.bfloat16), before.astype(jnp.bfloat16), preferred_element_type=jnp.float32
    ).astype(jnp.int32)
    picked = (
        position[:, None, :] == jnp.arange(ROW_LIMIT, dtype=jnp.int32)[None, :, None]
    ) & chosen[:, None, :]
    picker = picked.astype(jnp.bfloat16).reshape(2 * ROW_LIMIT, tok_rows)
    weights = jnp.where(picked, factor[:, None, :], 0.0).reshape(2 * ROW_LIMIT, tok_rows)

    packed = jnp.dot(picker, arrived, preferred_element_type=jnp.float32).astype(jnp.bfloat16)
    same, other = packed[:ROW_LIMIT], packed[ROW_LIMIT:]
    ahead = jnp.where(low, same, other)
    behind = jnp.where(low, other, same)

    sources = [
        same,
        along_chips(ahead, 4),
        along_chips(other, 8),
        along_chips(behind, -4),
    ]
    ring = jnp.stack(sources + sources[:3])
    chunk = lax.dynamic_slice_in_dim(ring, cut, 4, axis=0)

    def hidden_part(m):
        rows = chunk if m == 0 else swapped_chips(chunk, m)
        both = jnp.concatenate([rows, other_core(rows)], axis=1)
        flat = both.reshape(8 * ROW_LIMIT, width)
        part = jnp.dot(flat, up, preferred_element_type=jnp.float32).astype(jnp.bfloat16)
        return part.reshape(4, 2 * ROW_LIMIT, up.shape[1])

    total = jnp.zeros((4, ROW_LIMIT, width), jnp.float32)
    for group in CHUNK_GROUPS:
        parts = jnp.concatenate([hidden_part(m) for m in group], axis=1)
        hidden = cut_sum([parts[b] for b in range(4)])
        active = jax.nn.gelu(hidden).astype(jnp.bfloat16)
        gathered = jnp.stack(cut_gather(active)).reshape(4 * len(group) * 2 * ROW_LIMIT, up.shape[1])
        out = jnp.dot(gathered, down, preferred_element_type=jnp.float32).astype(jnp.bfloat16)
        out = out.reshape(4, len(group), 2, ROW_LIMIT, width)
        for at, m in enumerate(group):
            both = out[:, at, 0].astype(jnp.float32) + other_core(out[:, at, 1]).astype(jnp.float32)
            if m == 0:
                total = total + both
            else:
                total = total + swapped_chips(both.astype(jnp.bfloat16), m).astype(jnp.float32)

    rounded = total.astype(jnp.bfloat16)
    ring = jnp.concatenate([rounded, rounded[:3]])
    aligned = lax.dynamic_slice_in_dim(ring, (4 - cut) % 4, 4, axis=0)
    home = aligned[0].astype(jnp.float32)
    from_ahead = along_chips(aligned[1], -4).astype(jnp.float32)
    from_far = along_chips(aligned[2], 8).astype(jnp.float32)
    from_behind = along_chips(aligned[3], 4).astype(jnp.float32)
    same_sum = home + jnp.where(low, from_ahead, from_behind)
    other_sum = from_far + jnp.where(low, from_behind, from_ahead)
    spread = jnp.dot(
        weights.T,
        jnp.concatenate([same_sum, other_sum]),
        precision=lax.Precision.HIGHEST,
        preferred_element_type=jnp.float32,
    )
    return (arrived.astype(jnp.float32) + spread).astype(jnp.bfloat16)[None]


def solution(mesh):
    placed = (
        P("segment", "expert", "cuts"),
        P("segment", "expert", None),
        P("segment", "expert", None),
        P("segment", "expert", None),
        P("segment", "expert"),
        P("segment", "expert"),
        P("segment", "expert", "cuts", None),
        P("segment", "expert", None, "cuts"),
    )
    return jax.shard_map(
        shards,
        mesh=mesh,
        in_specs=placed,
        out_specs=P("segment", "expert", "cuts"),
        check_vma=False,
    )
```

```python
import jax
import jax.numpy as jnp
from jax import lax
from jax.sharding import PartitionSpec as P

EXP_FLIGHT = 2
ROW_LIMIT = 56
CHUNK_GROUPS = ((2, 3), (0, 1))


def moved(value, axis, targets):
    return lax.ppermute(value, axis, list(enumerate(targets)))


def along_chips(value, by):
    count = lax.axis_size("expert")
    return moved(value, "expert", [(j + 2 * by) % count for j in range(count)])


def swapped_chips(value, mask):
    return moved(value, "expert", [j ^ (2 * mask) for j in range(lax.axis_size("expert"))])


def other_core(value):
    return moved(value, "expert", [j ^ 1 for j in range(lax.axis_size("expert"))])


def along_cuts(value, by):
    count = lax.axis_size("cuts")
    return moved(value, "cuts", [(i + by) % count for i in range(count)])


def cut_sum(blocks):
    from_left = along_cuts(blocks[1], 1)
    from_right = along_cuts(blocks[3], 3)
    from_far = along_cuts(blocks[2], 2)
    return sum(part.astype(jnp.float32) for part in (blocks[0], from_left, from_right, from_far))


def back_home(value, step):
    targets = []
    for j in range(lax.axis_size("expert")):
        for c in range(4):
            home = [j, (j - 8) % 32, j ^ 20, (j + 8) % 32][c]
            targets.append(home * 4 + (c + step) % 4)
    return moved(value, ("expert", "cuts"), targets)


def shards(activations, pred_routes, true_routes, gate_scores, mis_rows, mis_count, w_up, w_down):
    arrived = lax.ppermute(activations, "segment", [(i, (i + 1) % 4) for i in range(4)])[0]
    tok_rows, width = arrived.shape
    up = w_up[0, 0]
    downs = lax.all_gather(w_down[0, 0], "cuts")
    chip = lax.axis_index("expert") // 2
    cut = lax.axis_index("cuts")
    half = chip // 8
    low = (chip % 8) < 4

    scores = gate_scores[0]
    gate = scores / jnp.sum(scores, axis=1, keepdims=True)
    listing = mis_rows[0]
    in_use = jnp.arange(listing.shape[0], dtype=jnp.int32) < mis_count[0, 0]
    listed = jnp.any(
        (jnp.arange(tok_rows, dtype=jnp.int32)[:, None] == listing[None, :]) & in_use[None, :],
        axis=1,
    )
    routes = jnp.where(listed[:, None], true_routes[0], pred_routes[0])
    order = jnp.stack([half, 1 - half])
    named = routes[None, :, :] == order[:, None, None]
    chosen = jnp.any(named, axis=2)
    factor = jnp.sum(jnp.where(named, gate[None], 0.0), axis=2)
    before = jnp.arange(tok_rows)[:, None] < jnp.arange(tok_rows)[None, :]
    position = jnp.dot(
        chosen.astype(jnp.bfloat16), before.astype(jnp.bfloat16), preferred_element_type=jnp.float32
    ).astype(jnp.int32)
    picked = (
        position[:, None, :] == jnp.arange(ROW_LIMIT, dtype=jnp.int32)[None, :, None]
    ) & chosen[:, None, :]
    picker = picked.astype(jnp.bfloat16).reshape(2 * ROW_LIMIT, tok_rows)
    weights = jnp.where(picked, factor[:, None, :], 0.0).reshape(2 * ROW_LIMIT, tok_rows)

    packed = jnp.dot(picker, arrived, preferred_element_type=jnp.float32).astype(jnp.bfloat16)
    same, other = packed[:ROW_LIMIT], packed[ROW_LIMIT:]
    ahead = jnp.where(low, same, other)
    behind = jnp.where(low, other, same)

    sources = [
        same,
        along_chips(ahead, 4),
        swapped_chips(other, 10),
        along_chips(behind, -4),
    ]
    ring = jnp.stack(sources + sources[:3])
    chunk = lax.dynamic_slice_in_dim(ring, cut, 4, axis=0)

    def hidden_part(m):
        rows = chunk if m == 0 else swapped_chips(chunk, m)
        both = jnp.concatenate([rows, other_core(rows)], axis=1)
        flat = both.reshape(8 * ROW_LIMIT, width)
        part = jnp.dot(flat, up, preferred_element_type=jnp.float32).astype(jnp.bfloat16)
        return part.reshape(4, 2 * ROW_LIMIT, up.shape[1])

    total = jnp.zeros((4, ROW_LIMIT, width), jnp.float32)
    for group in CHUNK_GROUPS:
        parts = jnp.concatenate([hidden_part(m) for m in group], axis=1)
        hidden = cut_sum([parts[b] for b in range(4)])
        active = jax.nn.gelu(hidden).astype(jnp.bfloat16)
        out = jnp.stack(
            [jnp.dot(active, downs[f], preferred_element_type=jnp.float32) for f in range(4)]
        ).astype(jnp.bfloat16)
        out = out.reshape(4, len(group), 2, ROW_LIMIT, width)
        both = out[:, :, 0].astype(jnp.float32) + other_core(out[:, :, 1]).astype(jnp.float32)
        for at, m in enumerate(group):
            if m == 0:
                total = total + both[:, at]
            else:
                total = total + swapped_chips(both[:, at].astype(jnp.bfloat16), m).astype(jnp.float32)

    rounded = total.astype(jnp.bfloat16)
    ring = jnp.concatenate([rounded, rounded[:3]])
    slices = lax.dynamic_slice_in_dim(ring, cut, 4, axis=0)
    same_sum = jnp.zeros((ROW_LIMIT, width), jnp.float32)
    other_sum = same_sum
    for step in range(4):
        part = back_home(slices[step], step).astype(jnp.float32)
        source = (cut - step) % 4
        is_same = (source == 0) | ((source == 1) & low) | ((source == 3) & ~low)
        same_sum = same_sum + jnp.where(is_same, part, 0.0)
        other_sum = other_sum + jnp.where(is_same, 0.0, part)
    spread = jnp.dot(
        weights.T,
        jnp.concatenate([same_sum, other_sum]),
        precision=lax.Precision.HIGHEST,
        preferred_element_type=jnp.float32,
    )
    return (arrived.astype(jnp.float32) + spread).astype(jnp.bfloat16)[None]


def solution(mesh):
    placed = (
        P("segment", "expert", "cuts"),
        P("segment", "expert", None),
        P("segment", "expert", None),
        P("segment", "expert", None),
        P("segment", "expert"),
        P("segment", "expert"),
        P("segment", "expert", "cuts", None),
        P("segment", "expert", None, "cuts"),
    )
    return jax.shard_map(
        shards,
        mesh=mesh,
        in_specs=placed,
        out_specs=P("segment", "expert", "cuts"),
        check_vma=False,
    )
```

```python
import jax
import jax.numpy as jnp
from jax import lax
from jax.sharding import PartitionSpec as P

EXP_FLIGHT = 2
ROW_LIMIT = 56
CHUNK_GROUPS = ((0, 1), (2, 3))


def moved(value, axis, targets):
    return lax.ppermute(value, axis, list(enumerate(targets)))


def along_chips(value, by):
    count = lax.axis_size("expert")
    return moved(value, "expert", [(j + 2 * by) % count for j in range(count)])


def swapped_chips(value, mask):
    return moved(value, "expert", [j ^ (2 * mask) for j in range(lax.axis_size("expert"))])


def other_core(value):
    return moved(value, "expert", [j ^ 1 for j in range(lax.axis_size("expert"))])


def along_cuts(value, by):
    count = lax.axis_size("cuts")
    return moved(value, "cuts", [(i + by) % count for i in range(count)])


def cut_sum(blocks):
    from_left = along_cuts(blocks[1], 1)
    from_right = along_cuts(blocks[3], 3)
    from_far = along_cuts(blocks[2], 2)
    return sum(part.astype(jnp.float32) for part in (blocks[0], from_left, from_right, from_far))


def cut_slices(own):
    from_right = along_cuts(own, 3)
    from_left = along_cuts(own, 1)
    part = own.shape[0] // 2
    far = [along_cuts(from_right[:part], 3), along_cuts(from_left[part:], 1)]
    return [[own], [from_right], far, [from_left]]


def back_home(value, step):
    targets = []
    for j in range(lax.axis_size("expert")):
        for c in range(4):
            home = [j, (j - 8) % 32, j ^ 20, (j + 8) % 32][c]
            targets.append(home * 4 + (c + step) % 4)
    return moved(value, ("expert", "cuts"), targets)


def shards(activations, pred_routes, true_routes, gate_scores, mis_rows, mis_count, w_up, w_down):
    arrived = lax.ppermute(activations, "segment", [(i, (i + 1) % 4) for i in range(4)])[0]
    tok_rows, width = arrived.shape
    up = jnp.concatenate([w_up[0, 0], other_core(w_up[0, 0])], axis=1)
    ff = w_down.shape[2]
    downs = [pieces + [other_core(piece) for piece in pieces] for pieces in cut_slices(w_down[0, 0])]
    chip = lax.axis_index("expert") // 2
    cut = lax.axis_index("cuts")
    half = chip // 8
    low = (chip % 8) < 4

    scores = gate_scores[0]
    gate = scores / jnp.sum(scores, axis=1, keepdims=True)
    listing = mis_rows[0]
    in_use = jnp.arange(listing.shape[0], dtype=jnp.int32) < mis_count[0, 0]
    listed = jnp.any(
        (jnp.arange(tok_rows, dtype=jnp.int32)[:, None] == listing[None, :]) & in_use[None, :],
        axis=1,
    )
    routes = jnp.where(listed[:, None], true_routes[0], pred_routes[0])
    order = jnp.stack([half, 1 - half])
    named = routes[None, :, :] == order[:, None, None]
    chosen = jnp.any(named, axis=2)
    factor = jnp.sum(jnp.where(named, gate[None], 0.0), axis=2)
    before = jnp.arange(tok_rows)[:, None] < jnp.arange(tok_rows)[None, :]
    position = jnp.dot(
        chosen.astype(jnp.bfloat16), before.astype(jnp.bfloat16), preferred_element_type=jnp.float32
    ).astype(jnp.int32)
    picked = (
        position[:, None, :] == jnp.arange(ROW_LIMIT, dtype=jnp.int32)[None, :, None]
    ) & chosen[:, None, :]
    picker = picked.astype(jnp.bfloat16).reshape(2 * ROW_LIMIT, tok_rows)
    weights = jnp.where(picked, factor[:, None, :], 0.0).reshape(2 * ROW_LIMIT, tok_rows)

    packed = jnp.dot(picker, arrived, preferred_element_type=jnp.float32).astype(jnp.bfloat16)
    same, other = packed[:ROW_LIMIT], packed[ROW_LIMIT:]
    ahead = jnp.where(low, same, other)
    behind = jnp.where(low, other, same)

    sources = [
        same,
        along_chips(ahead, 4),
        swapped_chips(other, 10),
        along_chips(behind, -4),
    ]
    ring = jnp.stack(sources + sources[:3])
    chunk = lax.dynamic_slice_in_dim(ring, cut, 4, axis=0)

    def hidden_part(m):
        rows = chunk if m == 0 else swapped_chips(chunk, m)
        flat = rows.reshape(4 * ROW_LIMIT, width)
        part = jnp.dot(flat, up, preferred_element_type=jnp.float32).astype(jnp.bfloat16)
        return part.reshape(4, ROW_LIMIT, 2 * ff)

    def times_down(active, pieces):
        low_unit, summed = 0, None
        for piece in pieces:
            high_unit = low_unit + piece.shape[0]
            term = jnp.dot(active[:, low_unit:high_unit], piece, preferred_element_type=jnp.float32)
            summed = term if summed is None else summed + term
            low_unit = high_unit
        return summed

    total = jnp.zeros((4, ROW_LIMIT, width), jnp.float32)
    for group in CHUNK_GROUPS:
        parts = jnp.concatenate([hidden_part(m) for m in group], axis=1)
        hidden = cut_sum([parts[b] for b in range(4)])
        active = jax.nn.gelu(hidden).astype(jnp.bfloat16)
        out = jnp.stack([times_down(active, pieces) for pieces in downs])
        out = out.reshape(4, len(group), ROW_LIMIT, width)
        for at, m in enumerate(group):
            if m == 0:
                total = total + out[:, at]
            else:
                total = total + swapped_chips(out[:, at].astype(jnp.bfloat16), m).astype(jnp.float32)

    rounded = total.astype(jnp.bfloat16)
    same_sum = jnp.zeros((ROW_LIMIT, width), jnp.float32)
    other_sum = same_sum
    for step in range(4):
        part = back_home(rounded[step], step).astype(jnp.float32)
        source = (cut - step) % 4
        is_same = (source == 0) | ((source == 1) & low) | ((source == 3) & ~low)
        same_sum = same_sum + jnp.where(is_same, part, 0.0)
        other_sum = other_sum + jnp.where(is_same, 0.0, part)
    spread = jnp.dot(
        weights.T,
        jnp.concatenate([same_sum, other_sum]),
        precision=lax.Precision.HIGHEST,
        preferred_element_type=jnp.float32,
    )
    return (arrived.astype(jnp.float32) + spread).astype(jnp.bfloat16)[None]


def solution(mesh):
    placed = (
        P("segment", "expert", "cuts"),
        P("segment", "expert", None),
        P("segment", "expert", None),
        P("segment", "expert", None),
        P("segment", "expert"),
        P("segment", "expert"),
        P("segment", "expert", "cuts", None),
        P("segment", "expert", None, "cuts"),
    )
    return jax.shard_map(
        shards,
        mesh=mesh,
        in_specs=placed,
        out_specs=P("segment", "expert", "cuts"),
        check_vma=False,
    )
```

```python
import jax
import jax.numpy as jnp
from jax import lax
from jax.sharding import PartitionSpec as P

EXP_FLIGHT = 2
ROW_LIMIT = 56
CHUNK_GROUPS = ((2, 3), (0, 1))


def moved(value, axis, targets):
    return lax.ppermute(value, axis, list(enumerate(targets)))


def along_chips(value, by):
    count = lax.axis_size("expert")
    return moved(value, "expert", [(j + 2 * by) % count for j in range(count)])


def swapped_chips(value, mask):
    return moved(value, "expert", [j ^ (2 * mask) for j in range(lax.axis_size("expert"))])


def other_core(value):
    return moved(value, "expert", [j ^ 1 for j in range(lax.axis_size("expert"))])


def after(value, *others):
    corners = [other[(0,) * other.ndim] * 0 for other in others]
    return value + sum(corners).astype(value.dtype)


def along_cuts(value, by):
    count = lax.axis_size("cuts")
    return moved(value, "cuts", [(i + by) % count for i in range(count)])


def cut_sum(blocks):
    from_left = along_cuts(blocks[1], 1)
    from_right = along_cuts(blocks[3], 3)
    from_far = along_cuts(blocks[2], 2)
    return sum(part.astype(jnp.float32) for part in (blocks[0], from_left, from_right, from_far))


def between_devices(value, target):
    count = lax.axis_size("expert")
    pairs = []
    for j in range(count):
        for c in range(4):
            to = target(j, c)
            if to is not None:
                pairs.append((j * 4 + c, to[0] * 4 + to[1] % 4))
    return lax.ppermute(value, ("expert", "cuts"), pairs)


def near_pieces(own):
    first = between_devices(own, lambda j, c: (j, c - 1) if j % 2 == 0 else (j, c + 1))
    second = between_devices(own, lambda j, c: (j ^ 1, c + 1) if j % 2 == 0 else (j ^ 1, c - 1))
    return first, second


def last_pieces(own, near, core):
    relayed = between_devices(near[1], lambda j, c: (j, c + 1) if j % 2 == 1 else None)
    sent = jnp.where(core == 0, near[1], own)
    last = between_devices(sent, lambda j, c: (j ^ 1, c - 1) if j % 2 == 0 else (j ^ 1, c))
    return jnp.where(core == 0, own, relayed), last


def slice_step(part, core):
    return (1, 3)[core] if part == 0 else (0, 2)[core]


def back_home(value, part, other):
    def target(j, c):
        k = (c + 2 * (j // 2 % 2)) % 4
        home = [j, (j - 8) % 32, j ^ 20, (j + 8) % 32][k]
        return home ^ other, c + slice_step(part, j % 2)

    return between_devices(value, target)


def shards(activations, pred_routes, true_routes, gate_scores, mis_rows, mis_count, w_up, w_down):
    arrived = lax.ppermute(activations, "segment", [(i, (i + 1) % 4) for i in range(4)])[0]
    tok_rows, width = arrived.shape
    core = lax.axis_index("expert") % 2
    up_other = other_core(w_up[0, 0])
    up = lax.optimization_barrier(jnp.concatenate([w_up[0, 0], up_other], axis=1))
    ff = w_down.shape[2]
    chip = lax.axis_index("expert") // 2
    cut = lax.axis_index("cuts")
    half = chip // 8
    low = (chip % 8) < 4

    scores = gate_scores[0]
    gate = scores / jnp.sum(scores, axis=1, keepdims=True)
    listing = mis_rows[0]
    in_use = jnp.arange(listing.shape[0], dtype=jnp.int32) < mis_count[0, 0]
    listed = jnp.any(
        (jnp.arange(tok_rows, dtype=jnp.int32)[:, None] == listing[None, :]) & in_use[None, :],
        axis=1,
    )
    routes = jnp.where(listed[:, None], true_routes[0], pred_routes[0])
    order = jnp.stack([half, 1 - half])
    named = routes[None, :, :] == order[:, None, None]
    chosen = jnp.any(named, axis=2)
    factor = jnp.sum(jnp.where(named, gate[None], 0.0), axis=2)
    before = jnp.arange(tok_rows)[:, None] < jnp.arange(tok_rows)[None, :]
    position = jnp.dot(
        chosen.astype(jnp.bfloat16), before.astype(jnp.bfloat16), preferred_element_type=jnp.float32
    ).astype(jnp.int32)
    picked = (
        position[:, None, :] == jnp.arange(ROW_LIMIT, dtype=jnp.int32)[None, :, None]
    ) & chosen[:, None, :]
    picker = picked.astype(jnp.bfloat16).reshape(2 * ROW_LIMIT, tok_rows)
    weights = jnp.where(picked, factor[:, None, :], 0.0).reshape(2 * ROW_LIMIT, tok_rows)

    near = near_pieces(w_down[0, 0])
    last = last_pieces(w_down[0, 0], near, core)
    packed = jnp.dot(picker, arrived, preferred_element_type=jnp.float32).astype(jnp.bfloat16)
    packed = after(packed, up_other)
    same, other = packed[:ROW_LIMIT], packed[ROW_LIMIT:]
    ahead = jnp.where(low, same, other)
    behind = jnp.where(low, other, same)

    sources = [
        same,
        along_chips(ahead, 4),
        swapped_chips(other, 10),
        along_chips(behind, -4),
    ]
    first = (cut + 2 * (chip % 2)) % 4
    numbers = ((first + jnp.arange(4)) % 4)[:, None, None]
    chunk = sum(jnp.where(numbers == k, rows[None], 0) for k, rows in enumerate(sources))
    chunk = after(chunk, near[0], near[1])

    def hidden_part(m):
        rows = chunk if m == 0 else swapped_chips(chunk, m)
        flat = rows.reshape(4 * ROW_LIMIT, width)
        part = jnp.dot(flat, up, preferred_element_type=jnp.float32).astype(jnp.bfloat16)
        return part.reshape(4, ROW_LIMIT, 2 * ff)

    def times_down(own_units, other_units):
        core_units = jnp.where(core == 0, own_units, other_units), jnp.where(core == 0, other_units, own_units)
        terms = [(own_units, near[0]), (other_units, near[1])], list(zip(core_units, last))
        dots = [[jnp.dot(u, w, preferred_element_type=jnp.float32) for u, w in t] for t in terms]
        return jnp.stack([a + b for a, b in dots])

    hiddens = []
    for group in CHUNK_GROUPS:
        parts = jnp.concatenate([hidden_part(m) for m in group], axis=1)
        hiddens.append(cut_sum([parts[b] for b in range(4)]))

    total = jnp.zeros((2, 2, ROW_LIMIT, width), jnp.float32)
    for group, hidden in zip(CHUNK_GROUPS, hiddens):
        active = jax.nn.gelu(hidden).astype(jnp.bfloat16)
        swapped = other_core(active)
        own_units = jnp.concatenate([active[:, :ff], swapped[:, ff:]])
        other_units = jnp.concatenate([active[:, ff:], swapped[:, :ff]])
        if 2 in group and 0 not in group:
            own_units = after(own_units, hiddens[1])
        out = times_down(own_units, other_units).reshape(2, 2, len(group), ROW_LIMIT, width)
        for at, m in enumerate(group):
            if m == 0:
                total = total + out[:, :, at]
            else:
                sent = out[:, :, at].astype(jnp.bfloat16)
                total = total + swapped_chips(sent, m).astype(jnp.float32)

    rounded = total.astype(jnp.bfloat16)
    same_sum = jnp.zeros((ROW_LIMIT, width), jnp.float32)
    other_sum = same_sum
    for part in range(2):
        for other in range(2):
            rows = back_home(rounded[part, other], part, other).astype(jnp.float32)
            step = jnp.where(core ^ other == 0, slice_step(part, 0), slice_step(part, 1))
            source = (first - step) % 4
            is_same = (source == 0) | ((source == 1) & low) | ((source == 3) & ~low)
            same_sum = same_sum + jnp.where(is_same, rows, 0.0)
            other_sum = other_sum + jnp.where(is_same, 0.0, rows)
    spread = jnp.dot(
        weights.T,
        jnp.concatenate([same_sum, other_sum]),
        precision=lax.Precision.HIGHEST,
        preferred_element_type=jnp.float32,
    )
    return (arrived.astype(jnp.float32) + spread).astype(jnp.bfloat16)[None]


def solution(mesh):
    placed = (
        P("segment", "expert", "cuts"),
        P("segment", "expert", None),
        P("segment", "expert", None),
        P("segment", "expert", None),
        P("segment", "expert"),
        P("segment", "expert"),
        P("segment", "expert", "cuts", None),
        P("segment", "expert", None, "cuts"),
    )
    return jax.shard_map(
        shards,
        mesh=mesh,
        in_specs=placed,
        out_specs=P("segment", "expert", "cuts"),
        check_vma=False,
    )
```

```python
import jax
import jax.numpy as jnp
from jax import lax
from jax.sharding import PartitionSpec as P

EXP_FLIGHT = 2
ROW_LIMIT = 56
CHUNK_GROUPS = ((2, 3), (0, 1))


def moved(value, axis, targets):
    return lax.ppermute(value, axis, list(enumerate(targets)))


def along_chips(value, by):
    count = lax.axis_size("expert")
    return moved(value, "expert", [(j + 2 * by) % count for j in range(count)])


def swapped_chips(value, mask):
    return moved(value, "expert", [j ^ (2 * mask) for j in range(lax.axis_size("expert"))])


def other_core(value):
    return moved(value, "expert", [j ^ 1 for j in range(lax.axis_size("expert"))])


def after(value, *others):
    corners = [other[(0,) * other.ndim] * 0 for other in others]
    return value + sum(corners).astype(value.dtype)


def along_cuts(value, by):
    count = lax.axis_size("cuts")
    return moved(value, "cuts", [(i + by) % count for i in range(count)])


def cut_sum(blocks):
    part = blocks[2].shape[0] // 2
    from_left = along_cuts(blocks[2][:part], 1).astype(jnp.float32)
    from_right = along_cuts(blocks[2][part:], 3).astype(jnp.float32)
    added = (blocks[1][:part] + from_left).astype(jnp.bfloat16)
    to_right = jnp.concatenate([added, blocks[1][part:]])
    added = (blocks[3][part:] + from_right).astype(jnp.bfloat16)
    to_left = jnp.concatenate([blocks[3][:part], added])
    arrivals = [along_cuts(to_right, 1), along_cuts(to_left, 3)]
    return blocks[0] + sum(part.astype(jnp.float32) for part in arrivals)


def between_devices(value, target):
    count = lax.axis_size("expert")
    pairs = []
    for j in range(count):
        for c in range(4):
            to = target(j, c)
            if to is not None:
                pairs.append((j * 4 + c, to[0] * 4 + to[1] % 4))
    return lax.ppermute(value, ("expert", "cuts"), pairs)


def near_pieces(own):
    first = between_devices(own, lambda j, c: (j, c - 1) if j % 2 == 0 else (j, c + 1))
    second = between_devices(own, lambda j, c: (j ^ 1, c + 1) if j % 2 == 0 else (j ^ 1, c - 1))
    return first, second


def last_pieces(own, near, core):
    relayed = between_devices(near[1], lambda j, c: (j, c + 1) if j % 2 == 1 else None)
    sent = jnp.where(core == 0, near[1], own)
    last = between_devices(sent, lambda j, c: (j ^ 1, c - 1) if j % 2 == 0 else (j ^ 1, c))
    return jnp.where(core == 0, own, relayed), last


def slice_step(part, core):
    return (1, 3)[core] if part == 0 else (0, 2)[core]


def back_home(value, part, other):
    def target(j, c):
        k = (c + 2 * (j // 2 % 2)) % 4
        home = [j, (j - 8) % 32, j ^ 20, (j + 8) % 32][k]
        return home ^ other, c + slice_step(part, j % 2)

    return between_devices(value, target)


def shards(activations, pred_routes, true_routes, gate_scores, mis_rows, mis_count, w_up, w_down):
    arrived = lax.ppermute(activations, "segment", [(i, (i + 1) % 4) for i in range(4)])[0]
    tok_rows, width = arrived.shape
    core = lax.axis_index("expert") % 2
    up_other = other_core(w_up[0, 0])
    up = lax.optimization_barrier(jnp.concatenate([w_up[0, 0], up_other], axis=1))
    ff = w_down.shape[2]
    chip = lax.axis_index("expert") // 2
    cut = lax.axis_index("cuts")
    half = chip // 8
    low = (chip % 8) < 4

    scores = gate_scores[0]
    gate = scores / jnp.sum(scores, axis=1, keepdims=True)
    listing = mis_rows[0]
    in_use = jnp.arange(listing.shape[0], dtype=jnp.int32) < mis_count[0, 0]
    listed = jnp.any(
        (jnp.arange(tok_rows, dtype=jnp.int32)[:, None] == listing[None, :]) & in_use[None, :],
        axis=1,
    )
    routes = jnp.where(listed[:, None], true_routes[0], pred_routes[0])
    order = jnp.stack([half, 1 - half])
    named = routes[None, :, :] == order[:, None, None]
    chosen = jnp.any(named, axis=2)
    factor = jnp.sum(jnp.where(named, gate[None], 0.0), axis=2)
    before = jnp.arange(tok_rows)[:, None] < jnp.arange(tok_rows)[None, :]
    position = jnp.dot(
        chosen.astype(jnp.bfloat16), before.astype(jnp.bfloat16), preferred_element_type=jnp.float32
    ).astype(jnp.int32)
    picked = (
        position[:, None, :] == jnp.arange(ROW_LIMIT, dtype=jnp.int32)[None, :, None]
    ) & chosen[:, None, :]
    picker = picked.astype(jnp.bfloat16).reshape(2 * ROW_LIMIT, tok_rows)
    weights = jnp.where(picked, factor[:, None, :], 0.0).reshape(2 * ROW_LIMIT, tok_rows)

    near = near_pieces(w_down[0, 0])
    last = last_pieces(w_down[0, 0], near, core)
    packed = jnp.dot(picker, arrived, preferred_element_type=jnp.float32).astype(jnp.bfloat16)
    packed = after(packed, up_other)
    same, other = packed[:ROW_LIMIT], packed[ROW_LIMIT:]
    ahead = jnp.where(low, same, other)
    behind = jnp.where(low, other, same)

    sources = [
        same,
        along_chips(ahead, 4),
        swapped_chips(other, 10),
        along_chips(behind, -4),
    ]
    first = (cut + 2 * (chip % 2)) % 4
    numbers = ((first + jnp.arange(4)) % 4)[:, None, None]
    chunk = sum(jnp.where(numbers == k, rows[None], 0) for k, rows in enumerate(sources))
    chunk = after(chunk, near[0], near[1])
    arrivals = []

    def hidden_part(m):
        rows = chunk if m == 0 else swapped_chips(chunk, m)
        arrivals.append(rows)
        if m == 0:
            rows = after(rows, arrivals[0])
        flat = rows.reshape(4 * ROW_LIMIT, width)
        part = jnp.dot(flat, up, preferred_element_type=jnp.float32).astype(jnp.bfloat16)
        return part.reshape(4, ROW_LIMIT, 2 * ff)

    def times_down(own_units, other_units):
        core_units = jnp.where(core == 0, own_units, other_units), jnp.where(core == 0, other_units, own_units)
        terms = [(own_units, near[0]), (other_units, near[1])], list(zip(core_units, last))
        dots = [[jnp.dot(u, w, preferred_element_type=jnp.float32) for u, w in t] for t in terms]
        return jnp.stack([a + b for a, b in dots])

    hiddens = []
    for group in CHUNK_GROUPS:
        parts = jnp.concatenate([hidden_part(m) for m in group], axis=1)
        hiddens.append(cut_sum([parts[b] for b in range(4)]))

    total = jnp.zeros((2, 2, ROW_LIMIT, width), jnp.float32)
    for group, hidden in zip(CHUNK_GROUPS, hiddens):
        active = jax.nn.gelu(hidden).astype(jnp.bfloat16)
        swapped = other_core(active)
        own_units = jnp.concatenate([active[:, :ff], swapped[:, ff:]])
        other_units = jnp.concatenate([active[:, ff:], swapped[:, :ff]])
        out = times_down(own_units, other_units).reshape(2, 2, len(group), ROW_LIMIT, width)
        for at, m in enumerate(group):
            if m == 0:
                total = total + out[:, :, at]
            else:
                sent = out[:, :, at].astype(jnp.bfloat16)
                total = total + swapped_chips(sent, m).astype(jnp.float32)

    rounded = total.astype(jnp.bfloat16)
    same_sum = jnp.zeros((ROW_LIMIT, width), jnp.float32)
    other_sum = same_sum
    for part in range(2):
        for other in range(2):
            rows = back_home(rounded[part, other], part, other).astype(jnp.float32)
            step = jnp.where(core ^ other == 0, slice_step(part, 0), slice_step(part, 1))
            source = (first - step) % 4
            is_same = (source == 0) | ((source == 1) & low) | ((source == 3) & ~low)
            same_sum = same_sum + jnp.where(is_same, rows, 0.0)
            other_sum = other_sum + jnp.where(is_same, 0.0, rows)
    spread = jnp.dot(
        weights.T,
        jnp.concatenate([same_sum, other_sum]),
        precision=lax.Precision.HIGHEST,
        preferred_element_type=jnp.float32,
    )
    return (arrived.astype(jnp.float32) + spread).astype(jnp.bfloat16)[None]


def solution(mesh):
    placed = (
        P("segment", "expert", "cuts"),
        P("segment", "expert", None),
        P("segment", "expert", None),
        P("segment", "expert", None),
        P("segment", "expert"),
        P("segment", "expert"),
        P("segment", "expert", "cuts", None),
        P("segment", "expert", None, "cuts"),
    )
    return jax.shard_map(
        shards,
        mesh=mesh,
        in_specs=placed,
        out_specs=P("segment", "expert", "cuts"),
        check_vma=False,
    )
```

```python
import jax
import jax.numpy as jnp
from jax import lax
from jax.sharding import PartitionSpec as P

EXP_FLIGHT = 2
ROW_LIMIT = 56
CHUNK_GROUPS = ((2, 3), (0, 1))


def moved(value, axis, targets):
    return lax.ppermute(value, axis, list(enumerate(targets)))


def along_chips(value, by):
    count = lax.axis_size("expert")
    return moved(value, "expert", [(j + 2 * by) % count for j in range(count)])


def swapped_chips(value, mask):
    return moved(value, "expert", [j ^ (2 * mask) for j in range(lax.axis_size("expert"))])


def other_core(value):
    return moved(value, "expert", [j ^ 1 for j in range(lax.axis_size("expert"))])


def after(value, *others):
    corners = [other[(0,) * other.ndim] * 0 for other in others]
    return value + sum(corners).astype(value.dtype)


def along_cuts(value, by):
    count = lax.axis_size("cuts")
    return moved(value, "cuts", [(i + by) % count for i in range(count)])


def cut_sum(blocks):
    part = blocks[2].shape[0] // 2
    from_left = along_cuts(blocks[2][:part], 1).astype(jnp.float32)
    from_right = along_cuts(blocks[2][part:], 3).astype(jnp.float32)
    added = (blocks[1][:part] + from_left).astype(jnp.bfloat16)
    to_right = jnp.concatenate([added, blocks[1][part:]])
    added = (blocks[3][part:] + from_right).astype(jnp.bfloat16)
    to_left = jnp.concatenate([blocks[3][:part], added])
    arrivals = [along_cuts(to_right, 1), along_cuts(to_left, 3)]
    return blocks[0] + sum(part.astype(jnp.float32) for part in arrivals)


def between_devices(value, target):
    count = lax.axis_size("expert")
    pairs = []
    for j in range(count):
        for c in range(4):
            to = target(j, c)
            if to is not None:
                pairs.append((j * 4 + c, to[0] * 4 + to[1] % 4))
    return lax.ppermute(value, ("expert", "cuts"), pairs)


def near_pieces(own):
    first = between_devices(own, lambda j, c: (j, c - 1) if j % 2 == 0 else (j, c + 1))
    second = between_devices(own, lambda j, c: (j ^ 1, c + 1) if j % 2 == 0 else (j ^ 1, c - 1))
    return first, second


def last_pieces(own, near, core):
    relayed = between_devices(near[1], lambda j, c: (j, c + 1) if j % 2 == 1 else None)
    sent = jnp.where(core == 0, near[1], own)
    last = between_devices(sent, lambda j, c: (j ^ 1, c - 1) if j % 2 == 0 else (j ^ 1, c))
    return jnp.where(core == 0, own, relayed), last


def slice_step(part, core):
    return (1, 3)[core] if part == 0 else (0, 2)[core]


def back_home(value, part):
    def target(j, c):
        k = (c + 2 * (j // 2 % 2)) % 4
        home = [j, (j - 8) % 32, j ^ 20, (j + 8) % 32][k]
        return home, c + slice_step(part, j % 2)

    return between_devices(value, target)


def shards(activations, pred_routes, true_routes, gate_scores, mis_rows, mis_count, w_up, w_down):
    arrived = lax.ppermute(activations, "segment", [(i, (i + 1) % 4) for i in range(4)])[0]
    tok_rows, width = arrived.shape
    core = lax.axis_index("expert") % 2
    up_other = other_core(w_up[0, 0])
    up = lax.optimization_barrier(jnp.concatenate([w_up[0, 0], up_other], axis=1))
    ff = w_down.shape[2]
    chip = lax.axis_index("expert") // 2
    cut = lax.axis_index("cuts")
    half = chip // 8
    low = (chip % 8) < 4

    scores = gate_scores[0]
    gate = scores / jnp.sum(scores, axis=1, keepdims=True)
    listing = mis_rows[0]
    in_use = jnp.arange(listing.shape[0], dtype=jnp.int32) < mis_count[0, 0]
    listed = jnp.any(
        (jnp.arange(tok_rows, dtype=jnp.int32)[:, None] == listing[None, :]) & in_use[None, :],
        axis=1,
    )
    routes = jnp.where(listed[:, None], true_routes[0], pred_routes[0])
    order = jnp.stack([half, 1 - half])
    named = routes[None, :, :] == order[:, None, None]
    chosen = jnp.any(named, axis=2)
    factor = jnp.sum(jnp.where(named, gate[None], 0.0), axis=2)
    before = jnp.arange(tok_rows)[:, None] < jnp.arange(tok_rows)[None, :]
    position = jnp.dot(
        chosen.astype(jnp.bfloat16), before.astype(jnp.bfloat16), preferred_element_type=jnp.float32
    ).astype(jnp.int32)
    picked = (
        position[:, None, :] == jnp.arange(ROW_LIMIT, dtype=jnp.int32)[None, :, None]
    ) & chosen[:, None, :]
    picker = picked.astype(jnp.bfloat16).reshape(2 * ROW_LIMIT, tok_rows)
    weights = jnp.where(picked, factor[:, None, :], 0.0).reshape(2 * ROW_LIMIT, tok_rows)

    near = near_pieces(w_down[0, 0])
    last = last_pieces(w_down[0, 0], near, core)
    picker = after(picker, up_other)
    packed = jnp.dot(picker, arrived, preferred_element_type=jnp.float32).astype(jnp.bfloat16)
    same, other = packed[:ROW_LIMIT], packed[ROW_LIMIT:]
    ahead = jnp.where(low, same, other)
    behind = jnp.where(low, other, same)

    sources = [
        same,
        along_chips(ahead, 4),
        swapped_chips(other, 10),
        along_chips(behind, -4),
    ]
    first = (cut + 2 * (chip % 2)) % 4
    ring = jnp.stack(sources + sources[:3])
    chunk = lax.dynamic_slice_in_dim(ring, first, 4, axis=0)
    near_chunk = after(chunk, near[0], near[1])
    arrivals = []

    def hidden_part(m):
        rows = chunk if m == 0 else swapped_chips(near_chunk if m == 1 else chunk, m)
        arrivals.append(rows)
        if m == 0:
            rows = after(rows, arrivals[0])
        flat = rows.reshape(4 * ROW_LIMIT, width)
        part = jnp.dot(flat, up, preferred_element_type=jnp.float32).astype(jnp.bfloat16)
        return part.reshape(4, ROW_LIMIT, 2 * ff)

    def times_down(own_units, other_units):
        core_units = jnp.where(core == 0, own_units, other_units), jnp.where(core == 0, other_units, own_units)
        terms = [(own_units, near[0]), (other_units, near[1])], list(zip(core_units, last))
        dots = [[jnp.dot(u, w, preferred_element_type=jnp.float32) for u, w in t] for t in terms]
        return jnp.stack([a + b for a, b in dots])

    hiddens = []
    for group in CHUNK_GROUPS:
        parts = jnp.concatenate([hidden_part(m) for m in group], axis=1)
        hiddens.append(cut_sum([parts[b] for b in range(4)]))

    total = jnp.zeros((2, 2, ROW_LIMIT, width), jnp.float32)
    for group, hidden in zip(CHUNK_GROUPS, hiddens):
        active = jax.nn.gelu(hidden).astype(jnp.bfloat16)
        swapped = other_core(active)
        own_units = jnp.concatenate([active[:, :ff], swapped[:, ff:]])
        other_units = jnp.concatenate([active[:, ff:], swapped[:, :ff]])
        out = times_down(own_units, other_units).reshape(2, 2, len(group), ROW_LIMIT, width)
        for at, m in enumerate(group):
            if m == 0:
                total = total + out[:, :, at]
            else:
                sent = out[:, :, at].astype(jnp.bfloat16)
                total = total + swapped_chips(sent, m).astype(jnp.float32)

    rounded = total.astype(jnp.bfloat16)
    came = jnp.stack([back_home(rounded[part], part) for part in range(2)])
    came = [came[:, 0], other_core(came[:, 1])]
    same_sum = jnp.zeros((ROW_LIMIT, width), jnp.float32)
    other_sum = same_sum
    for part in range(2):
        for other in range(2):
            rows = came[other][part].astype(jnp.float32)
            step = jnp.where(core ^ other == 0, slice_step(part, 0), slice_step(part, 1))
            source = (first - step) % 4
            is_same = (source == 0) | ((source == 1) & low) | ((source == 3) & ~low)
            same_sum = same_sum + jnp.where(is_same, rows, 0.0)
            other_sum = other_sum + jnp.where(is_same, 0.0, rows)
    spread = jnp.dot(
        weights.T,
        jnp.concatenate([same_sum, other_sum]),
        precision=lax.Precision.HIGHEST,
        preferred_element_type=jnp.float32,
    )
    return (arrived.astype(jnp.float32) + spread).astype(jnp.bfloat16)[None]


def solution(mesh):
    placed = (
        P("segment", "expert", "cuts"),
        P("segment", "expert", None),
        P("segment", "expert", None),
        P("segment", "expert", None),
        P("segment", "expert"),
        P("segment", "expert"),
        P("segment", "expert", "cuts", None),
        P("segment", "expert", None, "cuts"),
    )
    return jax.shard_map(
        shards,
        mesh=mesh,
        in_specs=placed,
        out_specs=P("segment", "expert", "cuts"),
        check_vma=False,
    )
```

```python
import jax
import jax.numpy as jnp
from jax import lax
from jax.sharding import PartitionSpec as P

EXP_FLIGHT = 2
ROW_LIMIT = 56
CHUNK_GROUPS = ((2, 3), (0, 1))


def moved(value, axis, targets):
    return lax.ppermute(value, axis, list(enumerate(targets)))


def along_chips(value, by):
    count = lax.axis_size("expert")
    return moved(value, "expert", [(j + 2 * by) % count for j in range(count)])


def swapped_chips(value, mask):
    return moved(value, "expert", [j ^ (2 * mask) for j in range(lax.axis_size("expert"))])


def other_core(value):
    return moved(value, "expert", [j ^ 1 for j in range(lax.axis_size("expert"))])


def after(value, *others):
    corners = [other[(0,) * other.ndim] * 0 for other in others]
    return value + sum(corners).astype(value.dtype)


def along_cuts(value, by):
    count = lax.axis_size("cuts")
    return moved(value, "cuts", [(i + by) % count for i in range(count)])


def cut_sum(blocks):
    part = blocks[2].shape[0] // 2
    from_left = along_cuts(blocks[2][:part], 1).astype(jnp.float32)
    from_right = along_cuts(blocks[2][part:], 3).astype(jnp.float32)
    added = (blocks[1][:part] + from_left).astype(jnp.bfloat16)
    to_right = jnp.concatenate([added, blocks[1][part:]])
    added = (blocks[3][part:] + from_right).astype(jnp.bfloat16)
    to_left = jnp.concatenate([blocks[3][:part], added])
    arrivals = [along_cuts(to_right, 1), along_cuts(to_left, 3)]
    return blocks[0] + sum(part.astype(jnp.float32) for part in arrivals)


def between_devices(value, target):
    count = lax.axis_size("expert")
    pairs = []
    for j in range(count):
        for c in range(4):
            to = target(j, c)
            if to is not None:
                pairs.append((j * 4 + c, to[0] * 4 + to[1] % 4))
    return lax.ppermute(value, ("expert", "cuts"), pairs)


def near_pieces(own):
    first = between_devices(own, lambda j, c: (j, c - 1) if j % 2 == 0 else (j, c + 1))
    second = between_devices(own, lambda j, c: (j ^ 1, c + 1) if j % 2 == 0 else (j ^ 1, c - 1))
    return first, second


def last_pieces(own, near, core):
    relayed = between_devices(near[1], lambda j, c: (j, c + 1) if j % 2 == 1 else None)
    sent = jnp.where(core == 0, near[1], own)
    last = between_devices(sent, lambda j, c: (j ^ 1, c - 1) if j % 2 == 0 else (j ^ 1, c))
    return jnp.where(core == 0, own, relayed), last


def slice_step(part, core):
    return (1, 3)[core] if part == 0 else (0, 2)[core]


def back_home(value, part):
    def target(j, c):
        k = (c + 2 * (j // 2 % 2)) % 4
        home = [j, (j - 8) % 32, j ^ 20, (j + 8) % 32][k]
        return home, c + slice_step(part, j % 2)

    return between_devices(value, target)


def shards(activations, pred_routes, true_routes, gate_scores, mis_rows, mis_count, w_up, w_down):
    arrived = lax.ppermute(activations, "segment", [(i, (i + 1) % 4) for i in range(4)])[0]
    tok_rows, width = arrived.shape
    core = lax.axis_index("expert") % 2
    up_other = other_core(w_up[0, 0])
    up = lax.optimization_barrier(jnp.concatenate([w_up[0, 0], up_other], axis=1))
    ff = w_down.shape[2]
    chip = lax.axis_index("expert") // 2
    cut = lax.axis_index("cuts")
    half = chip // 8
    low = (chip % 8) < 4

    scores = gate_scores[0]
    gate = scores / jnp.sum(scores, axis=1, keepdims=True)
    listing = mis_rows[0]
    in_use = jnp.arange(listing.shape[0], dtype=jnp.int32) < mis_count[0, 0]
    listed = jnp.any(
        (jnp.arange(tok_rows, dtype=jnp.int32)[:, None] == listing[None, :]) & in_use[None, :],
        axis=1,
    )
    routes = jnp.where(listed[:, None], true_routes[0], pred_routes[0])
    order = jnp.stack([half, 1 - half])
    named = routes[None, :, :] == order[:, None, None]
    chosen = jnp.any(named, axis=2)
    factor = jnp.sum(jnp.where(named, gate[None], 0.0), axis=2)
    before = jnp.arange(tok_rows)[:, None] < jnp.arange(tok_rows)[None, :]
    position = jnp.dot(
        chosen.astype(jnp.bfloat16), before.astype(jnp.bfloat16), preferred_element_type=jnp.float32
    ).astype(jnp.int32)
    picked = (
        position[:, None, :] == jnp.arange(ROW_LIMIT, dtype=jnp.int32)[None, :, None]
    ) & chosen[:, None, :]
    picker = picked.astype(jnp.bfloat16).reshape(2 * ROW_LIMIT, tok_rows)
    weights = jnp.where(picked, factor[:, None, :], 0.0).reshape(2 * ROW_LIMIT, tok_rows)

    near = near_pieces(w_down[0, 0])
    last = last_pieces(w_down[0, 0], near, core)
    picker = after(picker, up_other)
    packed = jnp.dot(picker, arrived, preferred_element_type=jnp.float32).astype(jnp.bfloat16)
    same, other = packed[:ROW_LIMIT], packed[ROW_LIMIT:]
    ahead = jnp.where(low, same, other)
    behind = jnp.where(low, other, same)

    sources = [
        same,
        along_chips(ahead, 4),
        swapped_chips(other, 10),
        along_chips(behind, -4),
    ]
    first = (cut + 2 * (chip % 2)) % 4
    ring = jnp.stack(sources + sources[:3])
    chunk = lax.dynamic_slice_in_dim(ring, first, 4, axis=0)
    near_chunk = after(chunk, near[0], near[1])
    arrivals = []

    def hidden_part(m):
        rows = chunk if m == 0 else swapped_chips(near_chunk if m == 1 else chunk, m)
        arrivals.append(rows)
        flat = rows.reshape(4 * ROW_LIMIT, width)
        part = jnp.dot(flat, up, preferred_element_type=jnp.float32).astype(jnp.bfloat16)
        part = part.reshape(4, ROW_LIMIT, 2 * ff)
        return after(part, arrivals[0]) if m == 0 else part

    def times_down(own_units, other_units):
        core_units = jnp.where(core == 0, own_units, other_units), jnp.where(core == 0, other_units, own_units)
        terms = [(own_units, near[0]), (other_units, near[1])], list(zip(core_units, last))
        dots = [[jnp.dot(u, w, preferred_element_type=jnp.float32) for u, w in t] for t in terms]
        return jnp.stack([a + b for a, b in dots])

    hiddens = []
    for group in CHUNK_GROUPS:
        parts = jnp.concatenate([hidden_part(m) for m in group], axis=1)
        hiddens.append(cut_sum([parts[b] for b in range(4)]))

    total = jnp.zeros((2, 2, ROW_LIMIT, width), jnp.float32)
    for group, hidden in zip(CHUNK_GROUPS, hiddens):
        active = jax.nn.gelu(hidden).astype(jnp.bfloat16)
        swapped = other_core(active)
        own_units = jnp.concatenate([active[:, :ff], swapped[:, ff:]])
        other_units = jnp.concatenate([active[:, ff:], swapped[:, :ff]])
        out = times_down(own_units, other_units).reshape(2, 2, len(group), ROW_LIMIT, width)
        for at, m in enumerate(group):
            if m == 0:
                total = total + out[:, :, at]
            else:
                sent = out[:, :, at].astype(jnp.bfloat16)
                total = total + swapped_chips(sent, m).astype(jnp.float32)

    rounded = total.astype(jnp.bfloat16)
    came = jnp.stack([back_home(rounded[part], part) for part in range(2)])
    came = [came[:, 0], other_core(came[:, 1])]
    same_sum = jnp.zeros((ROW_LIMIT, width), jnp.float32)
    other_sum = same_sum
    for part in range(2):
        for other in range(2):
            rows = came[other][part].astype(jnp.float32)
            step = jnp.where(core ^ other == 0, slice_step(part, 0), slice_step(part, 1))
            source = (first - step) % 4
            is_same = (source == 0) | ((source == 1) & low) | ((source == 3) & ~low)
            same_sum = same_sum + jnp.where(is_same, rows, 0.0)
            other_sum = other_sum + jnp.where(is_same, 0.0, rows)
    spread = jnp.dot(
        weights.T,
        jnp.concatenate([same_sum, other_sum]),
        precision=lax.Precision.HIGHEST,
        preferred_element_type=jnp.float32,
    )
    return (arrived.astype(jnp.float32) + spread).astype(jnp.bfloat16)[None]


def solution(mesh):
    placed = (
        P("segment", "expert", "cuts"),
        P("segment", "expert", None),
        P("segment", "expert", None),
        P("segment", "expert", None),
        P("segment", "expert"),
        P("segment", "expert"),
        P("segment", "expert", "cuts", None),
        P("segment", "expert", None, "cuts"),
    )
    return jax.shard_map(
        shards,
        mesh=mesh,
        in_specs=placed,
        out_specs=P("segment", "expert", "cuts"),
        check_vma=False,
    )
```
